32 devices in a mesh: row: 4 (over x, core), col: 8 (over z, y).
Axes of the slice: x: 2, y: 2, z: 4, core: 2. Of those that a mesh axis runs over, the one named last changes fastest.
Arguments:
- src_points: bfloat16 [1024, 256], P(('row', 'col')), may hold values from -16 to 16, as said below
- tgt_points: bfloat16 [1024, 256], P(('col', 'row')), may hold values from -16 to 16, as said below
- log_src: float32 [1024], P('row'), may hold values from -144 to 4, as said below
- log_tgt: float32 [1024], P('col'), may hold values from -4 to 4
- tgt_potential: float32 [1024], P('col'), may hold values from -7680 to 7680
Outputs:
- src_potential: float32 [1024], P('row')
- new_tgt_potential: float32 [1024], P('col')
- src_map: bfloat16 [1024, 256], P(('row', 'col'))
- tgt_map: bfloat16 [1024, 256], P(('col', 'row'))
The draws below stay inside these ranges and needn't reach their ends.
Inputs may be any that keep to these rules, and one draw needn't show every extreme that they name: `src_points`: coordinates of source codes. `tgt_points`: coordinates of target codes. `log_src`: unnormalised log-weights of the source points.
All inputs are finite; a program needn't handle non-finite values.
Results may differ from the reference program's by a relative error of at most 0.0033.
The reference program's roundings to bfloat16 on the way count: a program that leaves them out, or rounds other values in their place, can miss the bound.
Values may be sent and summed in bfloat16 or wider, within the bound.
A program may use at most 64 MiB of HBM per device.

```python
import math
import jax
import jax.numpy as jnp
from jax import lax

D = 256
NS = 1024
NT = 1024


def draw_src_points(key, part):
    key = jax.random.fold_in(key, 11)
    return jnp.clip(jax.random.normal(key, (NS, D), jnp.float32), -6.0, 6.0).astype(jnp.bfloat16)


def draw_tgt_points(key, part):
    key = jax.random.fold_in(key, 12)
    return jnp.clip(jax.random.normal(key, (NT, D), jnp.float32), -6.0, 6.0).astype(jnp.bfloat16)


def draw_tgt_potential(key, part):
    key = jax.random.fold_in(key, 13)
    epsilon = 0.1 * D
    return epsilon * jnp.clip(jax.random.normal(key, (NT,), jnp.float32), -4.0, 4.0)


def low_weights(key, scale):
    subkeys = jax.random.split(key, 2)
    count = max(1, NS // 32)
    order = jax.random.permutation(subkeys[0], NS)
    chosen = jnp.zeros((NS,), jnp.int32).at[order[:count]].set(1)
    depth = -128.0 - scale * jax.random.uniform(subkeys[1], (NS,), jnp.float32, 0.0, 1.0)
    return (chosen, depth)


def draw_log_src(key, part):
    key = jax.random.fold_in(key, 14)
    subkeys = jax.random.split(key, 2)
    chosen, depth = low_weights(subkeys[0], 12.0)
    drawn = jnp.clip(jax.random.normal(subkeys[1], (NS,), jnp.float32), -4.0, 4.0)
    return jnp.where(chosen == 1, depth, drawn)


def level_of(key, dims, pieces, smallest, largest):
    loudness = 1.0
    for position, shards_of in pieces:
        heights = jax.random.uniform(jax.random.fold_in(jax.random.fold_in(key, 6), position), (shards_of,), jnp.float32, smallest / len(pieces), largest / len(pieces))
        loudness = loudness * jnp.repeat(jnp.exp(heights), dims[position] // shards_of).reshape((-1,) + (1,) * (len(dims) - 1 - position))
    return loudness


def bell_draw(own_key, shape, scale, most, shards=(), held_as=jnp.bfloat16):
    drawn = scale * jax.random.normal(own_key, shape, jnp.float32)
    if shards:
        drawn = drawn * level_of(own_key, shape, shards, -0.22, 0.18)
    return jnp.clip(drawn, -most, most).astype(held_as)


def setup_inputs(seed: int = 0) -> dict:
    key_of = jax.random.split(jax.random.key(seed), 6)
    src_points = draw_src_points(jax.random.fold_in(key_of[5], 71), 0)
    tgt_points = draw_tgt_points(jax.random.fold_in(key_of[5], 71), 0)
    log_src = draw_log_src(jax.random.fold_in(key_of[5], 71), 0)
    log_tgt = bell_draw(key_of[3], (NT,), 1.0, 4.0, ((0, 8),), jnp.float32)
    tgt_potential = draw_tgt_potential(jax.random.fold_in(key_of[5], 71), 0)
    return {"src_points": src_points, "tgt_points": tgt_points, "log_src": log_src, "log_tgt": log_tgt, "tgt_potential": tgt_potential}


def cost_rows(src_block, targets, tgt_sq):
    src_sq = jnp.sum(jnp.square(src_block.astype(jnp.float32)), axis=1)
    inner = jnp.dot(src_block, targets.T, preferred_element_type=jnp.float32)
    return (src_sq[:, None] + tgt_sq[None, :] - 2.0 * inner).astype(jnp.bfloat16)


def widen(tile):
    return lax.optimization_barrier(tile).astype(jnp.float32)


def combine_lse(earlier, later):
    highest = jnp.maximum(earlier[0], later[0])
    return highest, earlier[1] * jnp.exp(earlier[0] - highest) + later[1] * jnp.exp(later[0] - highest)


def reference(src_points, tgt_points, log_src, log_tgt, tgt_potential):
    epsilon = 0.1 * D
    block_rows = math.gcd(NS, 1024)
    blocks = NS // block_rows
    tgt_sq = jnp.sum(jnp.square(tgt_points.astype(jnp.float32)), axis=1)
    src_blocks = src_points.reshape(blocks, block_rows, D)
    log_blocks = log_src.reshape(blocks, block_rows)

    def row_lse(src_block):
        costs = widen(cost_rows(src_block, tgt_points, tgt_sq))
        scores = log_tgt[None, :] + (tgt_potential[None, :] - costs) / epsilon
        highest = jnp.max(scores, axis=1)
        return highest + jnp.log(jnp.sum(jnp.exp(scores - highest[:, None]), axis=1))

    src_potential = -epsilon * lax.map(row_lse, src_blocks).reshape(NS)
    pot_blocks = src_potential.reshape(blocks, block_rows)

    def column_fold(running, element):
        src_block, log_block, pot_block = element
        costs = widen(cost_rows(src_block, tgt_points, tgt_sq))
        scores = log_block[:, None] + (pot_block[:, None] - costs) / epsilon
        highest = jnp.max(scores, axis=0)
        partial_pair = (highest, jnp.sum(jnp.exp(scores - highest[None, :]), axis=0))
        return combine_lse(running, partial_pair), None

    start = (jnp.full((NT,), -jnp.inf, jnp.float32), jnp.zeros((NT,), jnp.float32))
    (highest, totals), _ = lax.scan(column_fold, start, (src_blocks, log_blocks, pot_blocks))
    new_tgt_potential = -epsilon * (highest + jnp.log(totals))

    def map_fold(running, element):
        src_block, log_block, pot_block = element
        costs = widen(cost_rows(src_block, tgt_points, tgt_sq))
        scores = log_tgt[None, :] + (new_tgt_potential[None, :] - costs) / epsilon
        row_top = jnp.max(scores, axis=1)
        map_lse = row_top + jnp.log(jnp.sum(jnp.exp(scores - row_top[:, None]), axis=1))
        forward = jnp.exp(scores - map_lse[:, None]).astype(jnp.bfloat16)
        src_part = jnp.dot(forward, tgt_points, preferred_element_type=jnp.float32).astype(jnp.bfloat16)
        backward = jnp.exp(log_block[:, None] + (pot_block[:, None] - costs) / epsilon + new_tgt_potential[None, :] / epsilon).astype(jnp.bfloat16)
        return running + jnp.dot(backward.T, src_block, preferred_element_type=jnp.float32), src_part

    tgt_total, src_parts = lax.scan(map_fold, jnp.zeros((NT, D), jnp.float32), (src_blocks, log_blocks, pot_blocks))
    src_map = src_parts.reshape(NS, D)
    tgt_map = tgt_total.astype(jnp.bfloat16)
    return src_potential, new_tgt_potential, src_map, tgt_map
```

```python
import functools
import math

import jax
import jax.numpy as jnp
from jax import lax
from jax.experimental import pallas as pl
from jax.experimental.pallas import tpu as pltpu
from jax.sharding import PartitionSpec as P

MESH = pl.DeviceIdType.MESH
LOG2E = 1.0 / math.log(2.0)
LN2 = math.log(2.0)
NT_DIMS = (((1,), (1,)), ((), ()))
TN_DIMS = (((0,), (0,)), ((), ()))


def repeat(count, step):
    if count <= 8:
        for index in range(count):
            step(index)
    else:
        pl.loop(0, count)(step)


def block_of(index, size):
    start = index * size
    return pl.ds(start if isinstance(index, int) else pl.multiple_of(start, size), size)


def kernel(
    rows_n, cols_n,
    src_ref, tgt_ref, lsrc_ref, ltgt_ref, tpot_ref,
    spot_ref, npot_ref, smap_ref, tmap_ref,
    tgts, srcs, logs, cost, base, lse_cols, pair, pairs, part, parts,
    z_send, z_recv, y_send, y_recv, x_send, x_recv, c_send, c_recv,
    zs_send, zs_recv, ys_send, ys_recv, v_send, v_recv,
    m_send, m_recv, p_send, p_recv,
):
    row, col = lax.axis_index("row"), lax.axis_index("col")
    half_c, half_r = cols_n // 2, rows_n // 2
    zi, yi = col // 2, lax.rem(col, 2)
    xi, ci = row // 2, lax.rem(row, 2)
    own, width = tgt_ref.shape
    rows = cost.shape[0]
    targets = cost.shape[1]
    chunk = targets // half_c
    mine = targets // cols_n
    epsilon = 0.1 * width
    scale = LOG2E / epsilon

    def copy(src, dst, send, recv, to_row, to_col):
        return pltpu.make_async_remote_copy(
            src_ref=src, dst_ref=dst, send_sem=send, recv_sem=recv,
            device_id=(to_row, to_col), device_id_type=MESH,
        )

    barrier = pltpu.get_barrier_semaphore()
    for step in range(1, cols_n):
        pl.semaphore_signal(barrier, inc=1, device_id=(row, lax.rem(col + step, cols_n)), device_id_type=MESH)
    for step in range(1, rows_n):
        pl.semaphore_signal(barrier, inc=1, device_id=(lax.rem(row + step, rows_n), col), device_id_type=MESH)

    tgts[zi, yi, xi, ci] = tgt_ref[...]
    srcs[zi, yi] = src_ref[...]
    here = pl.ds(pl.multiple_of(col * mine, mine), mine)
    logs[0:1, here] = ltgt_ref[...]
    logs[1:2, here] = tpot_ref[...]
    pl.semaphore_wait(barrier, cols_n - 1 + rows_n - 1)

    other_y, other_c = 1 - yi, 1 - ci
    y_col = zi * 2 + other_y
    c_row = xi * 2 + other_c

    def z_copy(step):
        dst = lax.rem(zi + step, half_c)
        return copy(tgt_ref, tgts.at[zi, yi, xi, ci], z_send.at[step], z_recv.at[step], row, dst * 2 + yi)

    def zs_copy(step):
        dst = lax.rem(zi + step, half_c)
        return copy(src_ref, srcs.at[zi, yi], zs_send.at[step], zs_recv.at[step], row, dst * 2 + yi)

    def y_copy(step):
        which = lax.rem(zi - step + half_c, half_c)
        block = tgts.at[which, yi, xi, ci]
        return copy(block, block, y_send.at[step], y_recv.at[step], row, y_col)

    def ys_copy(step):
        which = lax.rem(zi - step + half_c, half_c)
        block = srcs.at[which, yi]
        return copy(block, block, ys_send.at[step], ys_recv.at[step], row, y_col)

    def x_copy(step, group):
        block = tgts.at[:, lax.rem(yi + group, 2), xi, ci]
        to_row = lax.rem(xi + step, half_r) * 2 + ci
        return copy(block, block, x_send.at[step, group], x_recv.at[step, group], to_row, col)

    def c_copy(step, group):
        which = lax.rem(xi - step + half_r, half_r)
        block = tgts.at[:, lax.rem(yi + group, 2), which, ci]
        return copy(block, block, c_send.at[step, group], c_recv.at[step, group], c_row, col)

    def v_copy(step):
        return copy(logs.at[:, here], logs.at[:, here], v_send.at[step], v_recv.at[step], row, lax.rem(col + step, cols_n))

    y_first = y_copy(0)
    y_first.start()
    for step in range(1, half_c):
        z_copy(step).start()
    ys_copy(0).start()
    for step in range(1, half_c):
        zs_copy(step).start()
    for step in range(1, cols_n):
        v_copy(step).start()

    for step in range(1, half_c):
        z_copy(step).wait_recv()
        y_copy(step).start()
    for step in range(1, half_r):
        x_copy(step, 0).start()
    c_copy(0, 0).start()
    for step in range(1, half_c):
        zs_copy(step).wait_recv()
        ys_copy(step).start()
    for step in range(half_c):
        y_copy(step).wait_recv()
    for step in range(1, half_r):
        x_copy(step, 1).start()
    c_copy(0, 1).start()
    for group in range(2):
        for step in range(1, half_r):
            x_copy(step, group).wait_recv()
            c_copy(step, group).start()
    for step in range(half_c):
        ys_copy(step).wait_recv()
    for step in range(1, cols_n):
        v_copy(step).wait_recv()
    for group in range(2):
        for step in range(half_r):
            c_copy(step, group).wait_recv()

    tall = math.gcd(rows, 256)
    blocks = tall // own
    flat = srcs.reshape(half_c * 2, own, width)

    def make_cost(index):
        span = block_of(index, chunk)
        tile = tgts[index].reshape(chunk, width)
        wide = tile.astype(jnp.float32)
        square = wide * wide
        high = square.astype(jnp.bfloat16)
        low = (square - high.astype(jnp.float32)).astype(jnp.bfloat16)
        ones = jnp.ones((16, width), jnp.bfloat16)
        dot = functools.partial(lax.dot_general, dimension_numbers=NT_DIMS, preferred_element_type=jnp.float32)
        tgt_sq = (dot(ones, high) + dot(ones, low))[0:1, :]

        def strip(part_index):
            src = flat[block_of(part_index, blocks)].reshape(tall, width)
            wide_src = src.astype(jnp.float32)
            src_sq = jnp.sum(wide_src * wide_src, axis=1, keepdims=True)
            value = (src_sq + tgt_sq) - 2.0 * dot(src, tile)
            cost[block_of(part_index, tall), span] = value.astype(jnp.bfloat16)

        repeat(rows // tall, strip)

    repeat(half_c, make_cost)

    forward_base = (logs[0:1, :] + logs[1:2, :] * (1.0 / epsilon)) * LOG2E

    def lse_rows(costs, offset):
        scores = offset - costs.astype(jnp.float32) * scale
        top = jnp.max(scores, axis=1, keepdims=True)
        mass = jnp.sum(jnp.exp2(scores - top), axis=1, keepdims=True)
        return top + jnp.log(mass) * LOG2E

    def first_pass(index):
        span = block_of(index, own)
        base[span, :] = jnp.broadcast_to(lse_rows(cost[span, :], forward_base), (own, base.shape[1]))

    repeat(rows // own, first_pass)
    spot_ref[...] = jnp.transpose(base[...])[0:1, :] * (-epsilon * LN2)
    source_logs = jnp.transpose(jnp.broadcast_to(lsrc_ref[...], (base.shape[1], rows)))
    base[...] = source_logs * LOG2E - base[...]

    def column_pass(index):
        span = block_of(index, chunk)
        scores = base[:, 0:1] - cost[:, span].astype(jnp.float32) * scale
        top = jnp.max(scores, axis=0, keepdims=True)
        pair[0:1, span] = top
        pair[1:2, span] = jnp.sum(jnp.exp2(scores - top), axis=0, keepdims=True)

    repeat(half_c, column_pass)

    def m_copy(step):
        return copy(pair, pairs.at[step - 1], m_send.at[step], m_recv.at[step], lax.rem(row + step, rows_n), col)

    for step in range(1, rows_n):
        m_copy(step).start()
    for step in range(1, rows_n):
        m_copy(step).wait_recv()
    tops = [pair[0:1, :]] + [pairs[step, 0:1, :] for step in range(rows_n - 1)]
    masses = [pair[1:2, :]] + [pairs[step, 1:2, :] for step in range(rows_n - 1)]
    highest = functools.reduce(jnp.maximum, tops)
    total = sum(mass * jnp.exp2(top - highest) for top, mass in zip(tops, masses))
    lse_cols[...] = highest + jnp.log(total) * LOG2E
    npot_ref[...] = lse_cols[0:1, here] * (-epsilon * LN2)

    backward = jnp.exp2(base[:, 0:1] - cost[:, here].astype(jnp.float32) * scale - lse_cols[0:1, here])
    sources = srcs[...].reshape(rows, width)
    partial = lax.dot_general(backward.astype(jnp.bfloat16), sources, TN_DIMS, preferred_element_type=jnp.float32)
    part[...] = partial.reshape(rows_n, own, width)

    def p_copy(step):
        to_row = lax.rem(row + step, rows_n)
        return copy(part.at[to_row], parts.at[step - 1], p_send.at[step], p_recv.at[step], to_row, col)

    for step in range(1, rows_n):
        p_copy(step).start()

    my_rows = pl.ds(pl.multiple_of(col * own, own), own)
    offset = logs[0:1, :] * LOG2E - lse_cols[...]
    map_lse = lse_rows(cost[my_rows, :], offset)
    smap = jnp.zeros((own, width), jnp.float32)

    def forward_part(index, running):
        span = block_of(index, chunk)
        move = logs[0:1, span] * LOG2E - lse_cols[0:1, span]
        weight = jnp.exp2((move - cost[my_rows, span].astype(jnp.float32) * scale) - map_lse)
        tile = tgts[index].reshape(chunk, width)
        return running + jnp.dot(weight.astype(jnp.bfloat16), tile, preferred_element_type=jnp.float32)

    if half_c <= 8:
        for index in range(half_c):
            smap = forward_part(index, smap)
    else:
        smap = lax.fori_loop(0, half_c, forward_part, smap)
    smap_ref[...] = smap.astype(jnp.bfloat16)

    for step in range(1, rows_n):
        p_copy(step).wait_recv()
    whole = part[row]
    for step in range(rows_n - 1):
        whole = whole + parts[step]
    tmap_ref[...] = whole.astype(jnp.bfloat16)

    for step in range(1, half_c):
        z_copy(step).wait_send()
        zs_copy(step).wait_send()
    for step in range(half_c):
        y_copy(step).wait_send()
        ys_copy(step).wait_send()
    for group in range(2):
        for step in range(half_r):
            if step:
                x_copy(step, group).wait_send()
            c_copy(step, group).wait_send()
    for step in range(1, cols_n):
        v_copy(step).wait_send()
    for step in range(1, rows_n):
        m_copy(step).wait_send()
        p_copy(step).wait_send()


def solution(mesh):
    rows_n, cols_n = mesh.shape["row"], mesh.shape["col"]
    half_c, half_r = cols_n // 2, rows_n // 2

    def body(src_points, tgt_points, log_src, log_tgt, tgt_potential):
        own, width = src_points.shape
        rows, mine = log_src.shape[0], log_tgt.shape[0]
        targets = mine * cols_n
        f32, bf16 = jnp.float32, jnp.bfloat16
        dma = pltpu.SemaphoreType.DMA
        vmem = pl.BlockSpec(memory_space=pltpu.VMEM)
        spot, npot, smap, tmap = pl.pallas_call(
            functools.partial(kernel, rows_n, cols_n),
            out_shape=(
                jax.ShapeDtypeStruct((1, rows), f32),
                jax.ShapeDtypeStruct((1, mine), f32),
                jax.ShapeDtypeStruct((own, width), bf16),
                jax.ShapeDtypeStruct((own, width), bf16),
            ),
            in_specs=[vmem] * 5,
            out_specs=(vmem,) * 4,
            scratch_shapes=[
                pltpu.VMEM((half_c, 2, half_r, 2, own, width), bf16),
                pltpu.VMEM((half_c, 2, own, width), bf16),
                pltpu.VMEM((2, targets), f32),
                pltpu.VMEM((rows, targets), bf16),
                pltpu.VMEM((rows, 128), f32),
                pltpu.VMEM((1, targets), f32),
                pltpu.VMEM((2, targets), f32),
                pltpu.VMEM((rows_n - 1, 2, targets), f32),
                pltpu.VMEM((rows_n, own, width), f32),
                pltpu.VMEM((rows_n - 1, own, width), f32),
                dma((half_c,)), dma((half_c,)),
                dma((half_c,)), dma((half_c,)),
                dma((half_r, 2)), dma((half_r, 2)),
                dma((half_r, 2)), dma((half_r, 2)),
                dma((half_c,)), dma((half_c,)),
                dma((half_c,)), dma((half_c,)),
                dma((cols_n,)), dma((cols_n,)),
                dma((rows_n,)), dma((rows_n,)),
                dma((rows_n,)), dma((rows_n,)),
            ],
            compiler_params=pltpu.CompilerParams(
                collective_id=0, has_side_effects=True, vmem_limit_bytes=56 * 1024 * 1024
            ),
        )(src_points, tgt_points, log_src[None, :], log_tgt[None, :], tgt_potential[None, :])
        return spot[0], npot[0], smap, tmap

    in_specs = (P(("row", "col"), None), P(("col", "row"), None), P("row"), P("col"), P("col"))
    out_specs = (P("row"), P("col"), P(("row", "col"), None), P(("col", "row"), None))
    return jax.shard_map(body, mesh=mesh, in_specs=in_specs, out_specs=out_specs, check_vma=False)
```

```python
import functools
import math

import jax
import jax.numpy as jnp
from jax import lax
from jax.experimental import pallas as pl
from jax.experimental.pallas import tpu as pltpu
from jax.sharding import PartitionSpec as P

MESH = pl.DeviceIdType.MESH
LOG2E = 1.0 / math.log(2.0)
LN2 = math.log(2.0)
NT_DIMS = (((1,), (1,)), ((), ()))
TN_DIMS = (((0,), (0,)), ((), ()))


def repeat(count, step):
    if count <= 8:
        for index in range(count):
            step(index)
    else:
        pl.loop(0, count)(step)


def block_of(index, size):
    start = index * size
    return pl.ds(start if isinstance(index, int) else pl.multiple_of(start, size), size)


def kernel(
    rows_n, cols_n,
    src_ref, tgt_ref, lsrc_ref, ltgt_ref, tpot_ref,
    spot_ref, npot_ref, smap_ref, tmap_ref,
    lsrc, tgts, srcs, logs, cost, base, lse_cols, pair, pairs, part, parts,
    z_send, z_recv, y_send, y_recv, x_send, x_recv, d_send, d_recv, c_send, c_recv,
    zs_send, zs_recv, ys_send, ys_recv, v_send, v_recv,
    m_send, m_recv, p_send, p_recv, in_sem,
):
    row, col = lax.axis_index("row"), lax.axis_index("col")
    half_c, half_r = cols_n // 2, rows_n // 2
    zi, yi = col // 2, lax.rem(col, 2)
    xi, ci = row // 2, lax.rem(row, 2)
    own, width = tgt_ref.shape
    rows = cost.shape[0]
    targets = cost.shape[1]
    chunk = targets // half_c
    mine = targets // cols_n
    epsilon = 0.1 * width
    scale = LOG2E / epsilon

    def copy(src, dst, send, recv, to_row, to_col):
        return pltpu.make_async_remote_copy(
            src_ref=src, dst_ref=dst, send_sem=send, recv_sem=recv,
            device_id=(to_row, to_col), device_id_type=MESH,
        )

    here = pl.ds(pl.multiple_of(col * mine, mine), mine)
    loads = (
        pltpu.make_async_copy(tgt_ref, tgts.at[zi, yi, xi, ci], in_sem.at[0]),
        pltpu.make_async_copy(src_ref, srcs.at[zi, yi], in_sem.at[1]),
        pltpu.make_async_copy(ltgt_ref, logs.at[0:1, here], in_sem.at[2]),
        pltpu.make_async_copy(tpot_ref, logs.at[1:2, here], in_sem.at[3]),
        pltpu.make_async_copy(lsrc_ref, lsrc, in_sem.at[4]),
    )
    other_y, other_c = 1 - yi, 1 - ci
    y_col = zi * 2 + other_y
    c_row = xi * 2 + other_c

    barrier = pltpu.get_barrier_semaphore()

    def greet(to_row, to_col):
        pl.semaphore_signal(barrier, inc=1, device_id=(to_row, to_col), device_id_type=MESH)

    for step in range(1, cols_n):
        greet(row, lax.rem(col + step, cols_n))
    for step in range(1, rows_n):
        greet(lax.rem(row + step, rows_n), col)
    for step in range(1, half_r):
        greet(lax.rem(xi + step, half_r) * 2 + ci, y_col)
    for load in loads:
        load.start()
    pl.semaphore_wait(barrier, cols_n - 1 + rows_n - 1 + half_r - 1)
    loads[0].wait()

    def z_copy(step):
        dst = lax.rem(zi + step, half_c)
        block = tgts.at[zi, yi, xi, ci]
        return copy(block, block, z_send.at[step], z_recv.at[step], row, dst * 2 + yi)

    def zs_copy(step):
        dst = lax.rem(zi + step, half_c)
        block = srcs.at[zi, yi]
        return copy(block, block, zs_send.at[step], zs_recv.at[step], row, dst * 2 + yi)

    def y_copy(step):
        which = lax.rem(zi - step + half_c, half_c)
        block = tgts.at[which, yi, xi, ci]
        return copy(block, block, y_send.at[step], y_recv.at[step], row, y_col)

    def ys_copy(step):
        which = lax.rem(zi - step + half_c, half_c)
        block = srcs.at[which, yi]
        return copy(block, block, ys_send.at[step], ys_recv.at[step], row, y_col)

    def x_copy(step, lag):
        block = tgts.at[lax.rem(zi - lag + half_c, half_c), yi, xi, ci]
        to_row = lax.rem(xi + step, half_r) * 2 + ci
        return copy(block, block, x_send.at[step, lag], x_recv.at[step, lag], to_row, col)

    def d_copy(step, lag):
        block = tgts.at[lax.rem(zi - lag + half_c, half_c), yi, xi, ci]
        to_row = lax.rem(xi + step, half_r) * 2 + ci
        return copy(block, block, d_send.at[step, lag], d_recv.at[step, lag], to_row, y_col)

    def c_copy(step, group):
        which = lax.rem(xi - step + half_r, half_r)
        block = tgts.at[:, lax.rem(yi + group, 2), which, ci]
        return copy(block, block, c_send.at[step, group], c_recv.at[step, group], c_row, col)

    def v_copy(step):
        return copy(logs.at[:, here], logs.at[:, here], v_send.at[step], v_recv.at[step], row, lax.rem(col + step, cols_n))

    def plane(lag):
        for step in range(1, half_r):
            d_copy(step, lag).start()
            x_copy(step, lag).start()
        y_copy(lag).start()

    for step in range(1, half_c):
        z_copy(step).start()
    plane(0)
    loads[1].wait()
    for step in range(1, half_c):
        zs_copy(step).start()
    ys_copy(0).start()
    for load in loads[2:]:
        load.wait()
    for step in range(1, cols_n):
        v_copy(step).start()

    for step in range(1, half_c):
        z_copy(step).wait_recv()
        plane(step)
    c_copy(0, 0).start()
    for step in range(1, half_c):
        zs_copy(step).wait_recv()
        ys_copy(step).start()
    for step in range(half_c):
        y_copy(step).wait_recv()
    c_copy(0, 1).start()
    for step in range(1, half_r):
        for lag in range(half_c):
            x_copy(step, lag).wait_recv()
        c_copy(step, 0).start()
    for step in range(1, half_r):
        for lag in range(half_c):
            d_copy(step, lag).wait_recv()
        c_copy(step, 1).start()
    for step in range(half_c):
        ys_copy(step).wait_recv()
    for step in range(1, cols_n):
        v_copy(step).wait_recv()
    for group in range(2):
        for step in range(half_r):
            c_copy(step, group).wait_recv()

    tall = math.gcd(rows, 256)
    blocks = tall // own
    flat = srcs.reshape(half_c * 2, own, width)

    def make_cost(index):
        span = block_of(index, chunk)
        tile = tgts[index].reshape(chunk, width)
        wide = tile.astype(jnp.float32)
        square = wide * wide
        high = square.astype(jnp.bfloat16)
        low = (square - high.astype(jnp.float32)).astype(jnp.bfloat16)
        ones = jnp.ones((16, width), jnp.bfloat16)
        dot = functools.partial(lax.dot_general, dimension_numbers=NT_DIMS, preferred_element_type=jnp.float32)
        tgt_sq = (dot(ones, high) + dot(ones, low))[0:1, :]

        def strip(part_index):
            src = flat[block_of(part_index, blocks)].reshape(tall, width)
            wide_src = src.astype(jnp.float32)
            src_sq = jnp.sum(wide_src * wide_src, axis=1, keepdims=True)
            value = (src_sq + tgt_sq) - 2.0 * dot(src, tile)
            cost[block_of(part_index, tall), span] = value.astype(jnp.bfloat16)

        repeat(rows // tall, strip)

    repeat(half_c, make_cost)

    forward_base = (logs[0:1, :] + logs[1:2, :] * (1.0 / epsilon)) * LOG2E

    def lse_rows(costs, offset):
        scores = offset - costs.astype(jnp.float32) * scale
        top = jnp.max(scores, axis=1, keepdims=True)
        mass = jnp.sum(jnp.exp2(scores - top), axis=1, keepdims=True)
        return top + jnp.log(mass) * LOG2E

    def first_pass(index):
        span = block_of(index, own)
        base[span, :] = jnp.broadcast_to(lse_rows(cost[span, :], forward_base), (own, base.shape[1]))

    repeat(rows // own, first_pass)
    spot_ref[...] = jnp.transpose(base[...])[0:1, :] * (-epsilon * LN2)
    source_logs = jnp.transpose(jnp.broadcast_to(lsrc[...], (base.shape[1], rows)))
    base[...] = source_logs * LOG2E - base[...]

    def column_pass(index):
        span = block_of(index, chunk)
        scores = base[:, 0:1] - cost[:, span].astype(jnp.float32) * scale
        top = jnp.max(scores, axis=0, keepdims=True)
        pair[0:1, span] = top
        pair[1:2, span] = jnp.sum(jnp.exp2(scores - top), axis=0, keepdims=True)

    repeat(half_c, column_pass)

    def m_copy(step):
        return copy(pair, pairs.at[step - 1], m_send.at[step], m_recv.at[step], lax.rem(row + step, rows_n), col)

    for step in range(1, rows_n):
        m_copy(step).start()
    for step in range(1, rows_n):
        m_copy(step).wait_recv()
    tops = [pair[0:1, :]] + [pairs[step, 0:1, :] for step in range(rows_n - 1)]
    masses = [pair[1:2, :]] + [pairs[step, 1:2, :] for step in range(rows_n - 1)]
    highest = functools.reduce(jnp.maximum, tops)
    total = sum(mass * jnp.exp2(top - highest) for top, mass in zip(tops, masses))
    lse_cols[...] = highest + jnp.log(total) * LOG2E
    npot_ref[...] = lse_cols[0:1, here] * (-epsilon * LN2)

    backward = jnp.exp2(base[:, 0:1] - cost[:, here].astype(jnp.float32) * scale - lse_cols[0:1, here])
    sources = srcs[...].reshape(rows, width)
    partial = lax.dot_general(backward.astype(jnp.bfloat16), sources, TN_DIMS, preferred_element_type=jnp.float32)
    part[...] = partial.reshape(rows_n, own, width)

    def p_copy(step):
        to_row = lax.rem(row + step, rows_n)
        return copy(part.at[to_row], parts.at[step - 1], p_send.at[step], p_recv.at[step], to_row, col)

    for step in range(1, rows_n):
        p_copy(step).start()

    my_rows = pl.ds(pl.multiple_of(col * own, own), own)
    offset = logs[0:1, :] * LOG2E - lse_cols[...]
    map_lse = lse_rows(cost[my_rows, :], offset)
    smap = jnp.zeros((own, width), jnp.float32)

    def forward_part(index, running):
        span = block_of(index, chunk)
        move = logs[0:1, span] * LOG2E - lse_cols[0:1, span]
        weight = jnp.exp2((move - cost[my_rows, span].astype(jnp.float32) * scale) - map_lse)
        tile = tgts[index].reshape(chunk, width)
        return running + jnp.dot(weight.astype(jnp.bfloat16), tile, preferred_element_type=jnp.float32)

    if half_c <= 8:
        for index in range(half_c):
            smap = forward_part(index, smap)
    else:
        smap = lax.fori_loop(0, half_c, forward_part, smap)
    smap_ref[...] = smap.astype(jnp.bfloat16)

    for step in range(1, rows_n):
        p_copy(step).wait_recv()
    whole = part[row]
    for step in range(rows_n - 1):
        whole = whole + parts[step]
    tmap_ref[...] = whole.astype(jnp.bfloat16)

    for step in range(1, half_c):
        z_copy(step).wait_send()
        zs_copy(step).wait_send()
    for step in range(half_c):
        y_copy(step).wait_send()
        ys_copy(step).wait_send()
        for jump in range(1, half_r):
            x_copy(jump, step).wait_send()
            d_copy(jump, step).wait_send()
    for group in range(2):
        for step in range(half_r):
            c_copy(step, group).wait_send()
    for step in range(1, cols_n):
        v_copy(step).wait_send()
    for step in range(1, rows_n):
        m_copy(step).wait_send()
        p_copy(step).wait_send()


def write_out(*refs):
    half = len(refs) // 2
    for src, dst in zip(refs[:half], refs[half:]):
        dst[...] = src[...]


def solution(mesh):
    rows_n, cols_n = mesh.shape["row"], mesh.shape["col"]
    half_c, half_r = cols_n // 2, rows_n // 2

    def body(src_points, tgt_points, log_src, log_tgt, tgt_potential):
        own, width = src_points.shape
        rows, mine = log_src.shape[0], log_tgt.shape[0]
        targets = mine * cols_n
        f32, bf16 = jnp.float32, jnp.bfloat16
        dma = pltpu.SemaphoreType.DMA
        vmem = pl.BlockSpec(memory_space=pltpu.VMEM)
        shapes = (
            jax.ShapeDtypeStruct((1, rows), f32),
            jax.ShapeDtypeStruct((1, mine), f32),
            jax.ShapeDtypeStruct((own, width), bf16),
            jax.ShapeDtypeStruct((own, width), bf16),
        )
        held = 2 * rows * targets + 2 * targets * width
        results = pl.pallas_call(
            functools.partial(kernel, rows_n, cols_n),
            out_shape=shapes,
            in_specs=[pl.BlockSpec(memory_space=pltpu.HBM)] * 5,
            out_specs=(vmem,) * 4,
            scratch_shapes=[
                pltpu.VMEM((1, rows), f32),
                pltpu.VMEM((half_c, 2, half_r, 2, own, width), bf16),
                pltpu.VMEM((half_c, 2, own, width), bf16),
                pltpu.VMEM((2, targets), f32),
                pltpu.VMEM((rows, targets), bf16),
                pltpu.VMEM((rows, 128), f32),
                pltpu.VMEM((1, targets), f32),
                pltpu.VMEM((2, targets), f32),
                pltpu.VMEM((rows_n - 1, 2, targets), f32),
                pltpu.VMEM((rows_n, own, width), f32),
                pltpu.VMEM((rows_n - 1, own, width), f32),
                dma((half_c,)), dma((half_c,)),
                dma((half_c,)), dma((half_c,)),
                dma((half_r, half_c)), dma((half_r, half_c)),
                dma((half_r, half_c)), dma((half_r, half_c)),
                dma((half_r, 2)), dma((half_r, 2)),
                dma((half_c,)), dma((half_c,)),
                dma((half_c,)), dma((half_c,)),
                dma((cols_n,)), dma((cols_n,)),
                dma((rows_n,)), dma((rows_n,)),
                dma((rows_n,)), dma((rows_n,)),
                dma((5,)),
            ],
            compiler_params=pltpu.CompilerParams(
                collective_id=0, has_side_effects=True, vmem_limit_bytes=min(56, 14 + 2 * held // 2**20) * 2**20
            ),
        )(src_points, tgt_points, log_src[None, :], log_tgt[None, :], tgt_potential[None, :])
        spot, npot, smap, tmap = pl.pallas_call(
            write_out, out_shape=shapes, in_specs=[vmem] * 4, out_specs=(vmem,) * 4
        )(*results)
        return spot[0], npot[0], smap, tmap

    in_specs = (P(("row", "col"), None), P(("col", "row"), None), P("row"), P("col"), P("col"))
    out_specs = (P("row"), P("col"), P(("row", "col"), None), P(("col", "row"), None))
    return jax.shard_map(body, mesh=mesh, in_specs=in_specs, out_specs=out_specs, check_vma=False)
```
